32 devices in a mesh: groups: 2 (over y), sector: 4 (over z), op: 4 (over x, core).
Axes of the slice: x: 2, y: 2, z: 4, core: 2. Of those that a mesh axis runs over, the one named last changes fastest.
Arguments:
- left_arrival: bfloat16 [256, 4, 256, 256], P(('groups', 'sector', 'op')), parts along dimension 0, may hold values from -0.1 to 0.15
- right_env: bfloat16 [8, 4, 8, 4, 256, 256], P('groups', 'op', None, 'sector'), parts along dimension 0, may hold values from -0.8 to 1.2
- op_charge: int32 [256], P('groups'), parts along dimension 0, may hold values from -1 to 1
- sector_dims: int32 [8], P(('groups', 'sector')), parts along dimension 0, may hold values from 192 to 256
- wavefunction: bfloat16 [8, 256, 256], P(('groups', 'sector')), parts along dimension 0, may hold values from -300 to 300
- onsite: float32 [8, 256, 256], P(('groups', 'sector')), parts along dimension 0, may hold values from 1 to 6
Outputs:
- last_image: float32 [8, 256, 256], P(('groups', 'sector')), parts along dimension 0
- correlation_matrix: float32 [6, 3], P('groups'), parts along dimension 0
The draws below stay inside these ranges and needn't reach their ends.
There are 2 independent parts, one for each index of `groups`. The reference program is written for one: setup_inputs(seed, part) draws one part's arguments, and reference() takes and returns one part's arrays. A program takes and returns all parts, laid end to end along the dimension named above; each array names one. Nothing has to cross between parts.
All inputs are finite; a program needn't handle non-finite values.
Results may differ from the reference program's by a relative error of at most 0.012.
Values may be sent and summed in bfloat16 or wider, within the bound.
A program may use at most 64 MiB of HBM per device.

```python
import math
import jax
import jax.numpy as jnp
from jax import lax

BLK = 256
NSEC = 4
OPS = 128
OPS_IN = 8
SGRP = 4
OGRP = 4


def noisy_blocks(key, leading, deviation, diagonal_mean):
    noise_key, factor_key = jax.random.split(key)
    shape = leading + (BLK, BLK)
    noise = jnp.clip(jax.random.normal(noise_key, shape, jnp.float32), -3.0, 3.0) * deviation
    factor = jax.random.uniform(factor_key, leading + (1, 1), jnp.float32, 0.6, 1.4)
    identity = jnp.eye(BLK, dtype=jnp.float32)
    return noise + diagonal_mean * factor * identity


def draw_left_arrival(key, part):
    key = jax.random.fold_in(key, 21)
    deviation = (BLK * OPS) ** (-0.5)
    blocks = noisy_blocks(key, (OPS, NSEC), deviation, 0.03)
    return blocks.astype(jnp.bfloat16)


def draw_right_env(key, part):
    key = jax.random.fold_in(key, 29)
    deviation = BLK ** (-0.5)
    blocks = noisy_blocks(key, (SGRP, OGRP, OPS_IN, NSEC), deviation, 0.3)
    return blocks.astype(jnp.bfloat16)


def draw_sector_dims(key, part):
    key = jax.random.fold_in(key, 7)
    states = jax.random.randint(key, (NSEC,), 3 * BLK // 4, BLK + 1)
    sector_index = jnp.arange(NSEC)
    states = jnp.where(sector_index == NSEC // 2, BLK, states)
    return jnp.where(sector_index == 0, 3 * BLK // 4, states).astype(jnp.int32)


def draw_wavefunction(key, part):
    key = jax.random.fold_in(key, 13)
    first_key, second_key, third_key = jax.random.split(key, 3)
    values = jnp.clip(jax.random.normal(first_key, (NSEC, BLK, BLK), jnp.float32), -6.0, 6.0)
    row_range = math.log(10.0)
    row_scale = jnp.exp(jax.random.uniform(second_key, (NSEC, BLK, 1), jnp.float32, 0.0, row_range))
    column_scale = jnp.exp(jax.random.uniform(third_key, (NSEC, 1, BLK), jnp.float32, 0.0, math.log(10.0)))
    sector_scale = 1.0 + jnp.arange(NSEC, dtype=jnp.float32)[:, None, None] / (NSEC - 1)
    return (values * row_scale * column_scale * sector_scale * 0.25).astype(jnp.bfloat16)


def plant(values, stream_key, smallest, high):
    place = [jax.random.randint(jax.random.fold_in(stream_key, axis), (), 0, length) for axis, length in enumerate(values.shape)]
    longest = values.shape.index(max(values.shape))
    beside = place[:longest] + [(place[longest] + 1) % values.shape[longest]] + place[longest + 1:]
    return values.at[tuple(place)].set(smallest).at[tuple(beside)].set(high)


def level_of(stream_key, extent, cuts, least, high):
    loudness = 1.0
    for axis_at, shards_of in cuts:
        steps = jax.random.uniform(jax.random.fold_in(jax.random.fold_in(stream_key, 6), axis_at), (shards_of,), jnp.float32, least / len(cuts), high / len(cuts))
        loudness = loudness * jnp.repeat(jnp.exp(steps), extent[axis_at] // shards_of).reshape((-1,) + (1,) * (len(extent) - 1 - axis_at))
    return loudness


def setup_inputs(seed: int = 0, part: int = 0) -> dict:
    keys = jax.random.split(jax.random.key(seed), 7)
    own_keys = jax.random.split(jax.random.fold_in(keys[6], part), 7)
    return {
        "left_arrival": draw_left_arrival(jax.random.fold_in(jax.random.fold_in(keys[6], part), 71), part),
        "right_env": draw_right_env(jax.random.fold_in(jax.random.fold_in(keys[6], part), 71), part),
        "op_charge": plant(jax.random.randint(own_keys[2], (OPS,), -1, 2), jax.random.fold_in(own_keys[2], 1), -1, 1).astype(jnp.int32),
        "sector_dims": draw_sector_dims(jax.random.fold_in(jax.random.fold_in(keys[6], part), 71), part),
        "wavefunction": draw_wavefunction(jax.random.fold_in(jax.random.fold_in(keys[6], part), 71), part),
        "onsite": jnp.clip(1.0 + 5.0 * jax.random.uniform(own_keys[5], (NSEC, BLK, BLK), jnp.float32) ** level_of(own_keys[5], (NSEC, BLK, BLK), ((0, 4),), -0.2, 0.2), 1.0, 6.0),
    }


def hamiltonian(vector, left_arrival, right_blocks, op_charge, onsite, sector_mask):
    padded = jnp.pad(vector, ((1, 1), (0, 0), (0, 0)))
    shifted = jnp.stack([padded[2:], padded[1:-1], padded[:-2]])

    def accumulate(aggregate_amounts, pieces):
        west_tensor, east_tensor, charge = pieces
        operand_state = lax.dynamic_index_in_dim(shifted, charge + 1, 0, keepdims=False)
        middle_portion = jnp.einsum('xzn,xne->xze', west_tensor.astype(jnp.float32), operand_state.astype(jnp.float32)).astype(jnp.bfloat16)
        return (aggregate_amounts + jnp.einsum('yib,yrb->yir', middle_portion.astype(jnp.float32), east_tensor.astype(jnp.float32)), None)
    aggregate_amounts, unused = lax.scan(accumulate, jnp.zeros(vector.shape, jnp.float32), (left_arrival, right_blocks, op_charge))
    return sector_mask * (onsite * vector.astype(jnp.float32) + aggregate_amounts)

def reference(left_arrival, right_env, op_charge, sector_dims, wavefunction, onsite):
    entries = NSEC * BLK * BLK
    right_blocks = right_env.reshape(OPS, NSEC, BLK, BLK)
    positions = jnp.arange(BLK, dtype=jnp.int32)
    inside = positions[None, :] < sector_dims[:, None]
    sector_mask = (inside[:, :, None] & inside[:, None, :]).astype(jnp.float32)
    masked = sector_mask * wavefunction.astype(jnp.float32)
    vectors = [(masked / jnp.sqrt(jnp.sum(masked * masked) / entries + 1e-06)).astype(jnp.bfloat16)]
    images = [hamiltonian(vectors[0], left_arrival, right_blocks, op_charge, onsite, sector_mask)]
    for section in range(2):
        current = vectors[section].astype(jnp.float32)
        image = images[section]
        rayleigh = jnp.sum(current * image) / jnp.sum(current * current)
        correction = (image - rayleigh * current) / (1.0 + jnp.abs(onsite - rayleigh))
        update = correction
        for earlier in range(section + 1):
            older = vectors[earlier].astype(jnp.float32)
            update = update - jnp.sum(older * correction) / jnp.sum(older * older) * older
        vectors.append((update / jnp.sqrt(jnp.sum(update * update) / entries + 1e-06)).astype(jnp.bfloat16))
        images.append(hamiltonian(vectors[-1], left_arrival, right_blocks, op_charge, onsite, sector_mask))
    correlation_values = [jnp.sum(vectors[row].astype(jnp.float32) * images[column]) for row in range(3) for column in range(3)]
    correlation_matrix = jnp.stack(correlation_values).reshape(3, 3) / entries
    return (images[2], correlation_matrix)
```

```python
import functools

import jax
import jax.numpy as jnp
from jax import lax
from jax.experimental import pallas as pl
from jax.experimental.pallas import tpu as pltpu
from jax.sharding import PartitionSpec as P

F32 = jnp.float32
BF16 = jnp.bfloat16
LANES = 128
MESH = pl.DeviceIdType.MESH


def fold(values):
    row = jnp.sum(values, axis=0, keepdims=True)
    total = row[:, :LANES]
    for start in range(LANES, row.shape[1], LANES):
        total = total + row[:, start : start + LANES]
    return total


def davidson_kernel(
    sectors, ops,
    left_ref, right_ref, charge_ref, dims_ref, wave_ref, onsite_ref,
    image_ref, corr_ref,
    lbuf, rbuf, pbuf, acc, v0, v1, v2, part_send, part_recv, full, tiles,
    left_local, right_local, left_send, left_recv, v_send, v_recv,
    part_send_sem, part_recv_sem, tile_send, tile_recv, full_send, full_recv,
):
    held = (v0, v1, v2)
    t = lax.axis_index("sector")
    q = lax.axis_index("op")
    me = t * ops + q
    peers = sectors * ops
    per = left_ref.shape[0]
    states = wave_ref.shape[1]
    quarter = states // ops
    blocks = sectors * per
    entries = sectors * states * states

    def rows_of(index):
        return pl.ds(pl.multiple_of(index * quarter, quarter), quarter)

    mine = rows_of(q)

    def device(s, o):
        return {"sector": s, "op": o}

    barrier = pltpu.get_barrier_semaphore()

    def greet(p, carry):
        other = lax.rem(me + p, peers)
        pl.semaphore_signal(
            barrier, inc=1, device_id=device(other // ops, lax.rem(other, ops)),
            device_id_type=MESH,
        )
        return carry

    lax.fori_loop(1, peers, greet, 0)

    right_copy = pltpu.make_async_copy(right_ref, rbuf, right_local)
    right_copy.start()
    own_copy = pltpu.make_async_copy(
        left_ref.at[:, t], lbuf.at[pl.ds(t * per, per)], left_local
    )
    own_copy.start()
    pl.semaphore_wait(barrier, peers - 1)

    def left_copy(k, p):
        target = lax.rem(t + p, sectors)
        return pltpu.make_async_remote_copy(
            src_ref=left_ref.at[k, target],
            dst_ref=lbuf.at[t * per + k],
            send_sem=left_send.at[p, k],
            recv_sem=left_recv.at[t, k],
            device_id=device(target, q),
            device_id_type=MESH,
        )

    def left_arrives(k, p):
        source = lax.rem(t + p, sectors)
        return source * per + k, pltpu.make_async_remote_copy(
            src_ref=left_ref.at[k, source],
            dst_ref=lbuf.at[source * per + k],
            send_sem=left_send.at[p, k],
            recv_sem=left_recv.at[source, k],
            device_id=device(source, q),
            device_id_type=MESH,
        )

    remote_blocks = per * (sectors - 1)

    def send_left(i, carry):
        left_copy(i // (sectors - 1), lax.rem(i, sectors - 1) + 1).start()
        return carry

    lax.fori_loop(0, remote_blocks, send_left, 0)

    def tile_copy(turn, p):
        other = lax.rem(me + p, peers)
        return other, pltpu.make_async_remote_copy(
            src_ref=tiles.at[turn, me],
            dst_ref=tiles.at[turn, me],
            send_sem=tile_send.at[turn, p],
            recv_sem=tile_recv.at[turn, me],
            device_id=device(other // ops, lax.rem(other, ops)),
            device_id_type=MESH,
        )

    def send_sums(turn, rows):
        rows = list(rows) + [jnp.zeros((8 - len(rows), LANES), F32)]
        tiles[turn, me] = jnp.concatenate(rows, axis=0)

        def step(p, carry):
            tile_copy(turn, p)[1].start()
            return carry

        lax.fori_loop(1, peers, step, 0)

    def take_sums(turn):
        def step(p, carry):
            other, copy = tile_copy(turn, p)
            pltpu.make_async_remote_copy(
                src_ref=tiles.at[turn, other],
                dst_ref=tiles.at[turn, other],
                send_sem=tile_send.at[turn, p],
                recv_sem=tile_recv.at[turn, other],
                device_id=device(other // ops, lax.rem(other, ops)),
                device_id_type=MESH,
            ).wait_recv()
            copy.wait_send()
            return carry

        lax.fori_loop(1, peers, step, 0)
        total = jnp.sum(jnp.sum(tiles[turn], axis=0), axis=1, keepdims=True)
        return [total[i : i + 1, :] for i in range(8)]

    def vector_copy(j, d, o, source):
        return pltpu.make_async_remote_copy(
            src_ref=held[j].at[1, mine],
            dst_ref=held[j].at[d + 1, rows_of(source)],
            send_sem=v_send.at[j, d + 1, o],
            recv_sem=v_recv.at[j, d + 1, source],
            device_id=device(t + d, o),
            device_id_type=MESH,
        )

    def each_reader(action):
        for d in (1, -1, 0):
            def run(d=d):
                def step(p, carry):
                    action(d, lax.rem(q + p, ops))
                    return carry

                lax.fori_loop(1 if d == 0 else 0, ops, step, 0)

            if d == 0:
                run()
            else:
                pl.when((t + d >= 0) & (t + d < sectors))(run)

    def send_vector(j, values):
        held[j][1, mine] = values
        each_reader(lambda d, o: vector_copy(j, d, o, q).start())

    def take_vector(j):
        each_reader(lambda d, o: vector_copy(j, -d, o, o).wait_recv())
        each_reader(lambda d, o: vector_copy(j, d, o, q).wait_send())

    for j in range(3):
        @pl.when(t == 0)
        def _(j=j):
            held[j][2] = jnp.zeros((states, states), BF16)

        @pl.when(t == sectors - 1)
        def _(j=j):
            held[j][0] = jnp.zeros((states, states), BF16)

    dims = dims_ref[0]
    row_at = lax.broadcasted_iota(jnp.int32, (quarter, states), 0) + q * quarter
    column_at = lax.broadcasted_iota(jnp.int32, (quarter, states), 1)
    mask = ((row_at < dims) & (column_at < dims)).astype(F32)
    onsite = onsite_ref[0, mine]

    masked = mask * wave_ref[0, mine].astype(F32)
    send_sums(0, [fold(masked * masked)])
    start_norm = take_sums(0)[0]
    vector = (masked / jnp.sqrt(start_norm / entries + 1e-06)).astype(BF16)
    send_vector(0, vector)
    right_copy.wait()
    own_copy.wait()

    def right_products(j):
        def step(i, carry):
            charge = charge_ref[(i // per * ops + q) * per + lax.rem(i, per)]
            pbuf[i] = lax.dot_general(
                held[j][charge + 1], rbuf[i], (((1,), (1,)), ((), ())),
                preferred_element_type=F32,
            ).astype(BF16)
            return carry

        lax.fori_loop(0, blocks, step, 0, unroll=4)

    def product(i):
        return jnp.dot(lbuf[i], pbuf[i], preferred_element_type=F32)

    group = 4 if blocks % 4 == 0 else 1

    def left_products(arriving):
        acc[...] = jnp.zeros_like(acc)
        if arriving:
            def own(k, carry):
                acc[...] += product(t * per + k)
                return carry

            lax.fori_loop(0, per, own, 0)

            def step(i, carry):
                at, copy = left_arrives(i // (sectors - 1), lax.rem(i, sectors - 1) + 1)
                copy.wait_recv()
                acc[...] += product(at)
                return carry

            lax.fori_loop(0, remote_blocks, step, 0)
        else:
            def step(i, carry):
                total = product(i * group)
                for n in range(1, group):
                    total = total + product(i * group + n)
                acc[...] += total
                return carry

            lax.fori_loop(0, blocks // group, step, 0)

    def part_copy(j, o, source):
        return pltpu.make_async_remote_copy(
            src_ref=part_send.at[j, rows_of(o)],
            dst_ref=part_recv.at[j, source],
            send_sem=part_send_sem.at[j, o],
            recv_sem=part_recv_sem.at[j, source],
            device_id=device(t, o),
            device_id_type=MESH,
        )

    def each_op(action):
        def step(p, carry):
            action(lax.rem(q + p, ops))
            return carry

        lax.fori_loop(1, ops, step, 0)

    def send_partial(j):
        part_send[j] = acc[...].astype(BF16)
        each_op(lambda o: part_copy(j, o, q).start())

    def take_partial(j, vector):
        part_recv[j, q] = part_send[j, mine]
        each_op(lambda o: part_copy(j, o, o).wait_recv())
        each_op(lambda o: part_copy(j, o, q).wait_send())
        total = acc[mine]
        own = part_recv[j, q].astype(F32)
        total = total + (jnp.sum(part_recv[j].astype(F32), axis=0) - own)
        return mask * (onsite * vector.astype(F32) + total)

    vectors = [vector]
    images = []
    norms = []
    ritz = []
    cross = []
    for j in range(3):
        current = vectors[j].astype(F32)
        take_vector(j)
        right_products(j)
        left_products(j == 0)
        send_partial(j)
        diagonal = onsite * current

        def overlap(i):
            whole = fold(held[i][1].astype(F32) * acc[...])
            return whole + fold(vectors[i].astype(F32) * diagonal)

        if j == 0:
            rows = [overlap(0), fold(current * current)]
        elif j == 1:
            first = vectors[0].astype(F32)
            rows = [
                overlap(1), fold(current * current), overlap(0),
                fold(current * images[0]), fold(first * current),
            ]
        else:
            rows = [
                overlap(2), overlap(0), overlap(1),
                fold(current * images[0]), fold(current * images[1]),
            ]
        send_sums(1 + 2 * j, rows)
        image = take_partial(j, vectors[j])
        images.append(image)
        if j == 2:
            break
        sums = take_sums(1 + 2 * j)
        ritz.append(sums)
        norms.append(sums[1])
        rayleigh = sums[0] / sums[1]
        correction = (image - rayleigh * current) / (1.0 + jnp.abs(onsite - rayleigh))
        send_sums(
            2 + 2 * j,
            [fold(correction * correction)]
            + [fold(older.astype(F32) * correction) for older in vectors],
        )
        seconds = take_sums(2 + 2 * j)
        length = seconds[0]
        update = correction
        factors = []
        for i in range(j + 1):
            factor = seconds[1 + i] / norms[i]
            factors.append(factor)
            update = update - factor * vectors[i].astype(F32)
            length = length - factor * seconds[1 + i]
        if j == 1:
            length = length + 2.0 * factors[0] * factors[1] * sums[4]
        length = jnp.maximum(length, 0.0)
        following = (update / jnp.sqrt(length / entries + 1e-06)).astype(BF16)
        vectors.append(following)
        send_vector(j + 1, following)

    full[mine] = images[2]

    def full_copy(o, source):
        return pltpu.make_async_remote_copy(
            src_ref=full.at[mine],
            dst_ref=full.at[rows_of(source)],
            send_sem=full_send.at[o],
            recv_sem=full_recv.at[source],
            device_id=device(t, o),
            device_id_type=MESH,
        )

    each_op(lambda o: full_copy(o, q).start())
    last = take_sums(5)
    values = [
        [ritz[0][0], ritz[1][2], last[1]],
        [ritz[1][3], ritz[1][0], last[2]],
        [last[3], last[4], last[0]],
    ]
    at_row = lax.broadcasted_iota(jnp.int32, (8, LANES), 0)
    at_column = lax.broadcasted_iota(jnp.int32, (8, LANES), 1)
    table = jnp.zeros((8, LANES), F32)
    for i in range(3):
        for n in range(3):
            table = jnp.where((at_row == i) & (at_column == n), values[i][n] / entries, table)
    corr_ref[...] = table[:3, :3]

    def sent_left(i, carry):
        left_copy(i // (sectors - 1), lax.rem(i, sectors - 1) + 1).wait_send()
        return carry

    lax.fori_loop(0, remote_blocks, sent_left, 0)
    each_op(lambda o: full_copy(o, o).wait_recv())
    each_op(lambda o: full_copy(o, q).wait_send())
    image_ref[0] = full[...]


def on_device(left_arrival, right_env, op_charge, sector_dims, wavefunction, onsite):
    sectors = lax.axis_size("sector")
    ops = lax.axis_size("op")
    per = left_arrival.shape[0]
    states = wavefunction.shape[1]
    blocks = sectors * per
    quarter = states // ops
    right = right_env.reshape(blocks, states, states)
    vmem = pl.BlockSpec(memory_space=pltpu.VMEM)
    smem = pl.BlockSpec(memory_space=pltpu.SMEM)
    anywhere = pl.BlockSpec(memory_space=pl.ANY)
    dma = pltpu.SemaphoreType.DMA
    return pl.pallas_call(
        functools.partial(davidson_kernel, sectors, ops),
        out_shape=(
            jax.ShapeDtypeStruct(wavefunction.shape, F32),
            jax.ShapeDtypeStruct((3, 3), F32),
        ),
        in_specs=[anywhere, anywhere, smem, smem, vmem, vmem],
        out_specs=(vmem, vmem),
        scratch_shapes=[
            pltpu.VMEM((blocks, states, states), BF16),
            pltpu.VMEM((blocks, states, states), BF16),
            pltpu.VMEM((blocks, states, states), BF16),
            pltpu.VMEM((states, states), F32),
            pltpu.VMEM((3, states, states), BF16),
            pltpu.VMEM((3, states, states), BF16),
            pltpu.VMEM((3, states, states), BF16),
            pltpu.VMEM((3, states, states), BF16),
            pltpu.VMEM((3, ops, quarter, states), BF16),
            pltpu.VMEM((states, states), F32),
            pltpu.VMEM((6, sectors * ops, 8, LANES), F32),
            dma,
            dma,
            dma((sectors, per)),
            dma((sectors, per)),
            dma((3, 3, ops)),
            dma((3, 3, ops)),
            dma((3, ops)),
            dma((3, ops)),
            dma((6, sectors * ops)),
            dma((6, sectors * ops)),
            dma((ops,)),
            dma((ops,)),
        ],
        compiler_params=pltpu.CompilerParams(
            collective_id=0, has_side_effects=True, vmem_limit_bytes=48 * 1024 * 1024
        ),
    )(left_arrival, right, op_charge, sector_dims, wavefunction, onsite)


def solution(mesh):
    in_specs = (
        P(("groups", "sector", "op"), None, None, None),
        P("groups", "op", None, "sector", None, None),
        P("groups"),
        P(("groups", "sector")),
        P(("groups", "sector"), None, None),
        P(("groups", "sector"), None, None),
    )
    out_specs = (P(("groups", "sector"), None, None), P("groups", None))
    return jax.shard_map(
        on_device, mesh=mesh, in_specs=in_specs, out_specs=out_specs, check_vma=False
    )
```

```python
import functools

import jax
import jax.numpy as jnp
from jax import lax
from jax.experimental import pallas as pl
from jax.experimental.pallas import tpu as pltpu
from jax.sharding import PartitionSpec as P

F32 = jnp.float32
BF16 = jnp.bfloat16
LANES = 128
MESH = pl.DeviceIdType.MESH


def fold(values):
    row = jnp.sum(values, axis=0, keepdims=True)
    total = row[:, :LANES]
    for start in range(LANES, row.shape[1], LANES):
        total = total + row[:, start : start + LANES]
    return total


def davidson_kernel(
    sectors, ops,
    left_ref, right_ref, charge_hbm, dims_hbm, wave_hbm, onsite_hbm,
    image_ref, corr_ref,
    charge_ref, dims_ref, wave_ref, onsite_ref, small_local, lbuf, rbuf, pbuf, acc, v0, v1, v2, part_send, part_recv, full, tiles,
    left_local, right_local, left_send, left_recv, v_send, v_recv,
    part_send_sem, part_recv_sem, tile_send, tile_recv, full_send, full_recv,
):
    held = (v0, v1, v2)
    t = lax.axis_index("sector")
    q = lax.axis_index("op")
    me = t * ops + q
    peers = sectors * ops
    per = left_ref.shape[0]
    states = wave_hbm.shape[1]
    quarter = states // ops
    blocks = sectors * per
    entries = sectors * states * states

    def rows_of(index):
        return pl.ds(pl.multiple_of(index * quarter, quarter), quarter)

    mine = rows_of(q)

    def device(s, o):
        return {"sector": s, "op": o}

    small_copies = [
        pltpu.make_async_copy(source, target, small_local.at[i])
        for i, (source, target) in enumerate((
            (dims_hbm, dims_ref), (wave_hbm, wave_ref), (onsite_hbm, onsite_ref),
            (charge_hbm, charge_ref),
        ))
    ]
    for copy in small_copies:
        copy.start()

    barrier = pltpu.get_barrier_semaphore()

    def greet(p, carry):
        other = lax.rem(me + p, peers)
        pl.semaphore_signal(
            barrier, inc=1, device_id=device(other // ops, lax.rem(other, ops)),
            device_id_type=MESH,
        )
        return carry

    lax.fori_loop(1, peers, greet, 0, unroll=peers <= 16)

    right_copy = pltpu.make_async_copy(right_ref, rbuf, right_local)
    right_copy.start()
    own_copy = pltpu.make_async_copy(
        left_ref.at[:, t], lbuf.at[pl.ds(t * per, per)], left_local
    )
    own_copy.start()

    def left_copy(k, p):
        target = lax.rem(t + p, sectors)
        return pltpu.make_async_remote_copy(
            src_ref=left_ref.at[k, target],
            dst_ref=lbuf.at[t * per + k],
            send_sem=left_send.at[p, k],
            recv_sem=left_recv.at[t, k],
            device_id=device(target, q),
            device_id_type=MESH,
        )

    def left_arrives(k, p):
        source = lax.rem(t + p, sectors)
        return source * per + k, pltpu.make_async_remote_copy(
            src_ref=left_ref.at[k, source],
            dst_ref=lbuf.at[source * per + k],
            send_sem=left_send.at[p, k],
            recv_sem=left_recv.at[source, k],
            device_id=device(source, q),
            device_id_type=MESH,
        )

    remote_blocks = per * (sectors - 1)

    def send_left(i, carry):
        left_copy(i // (sectors - 1), lax.rem(i, sectors - 1) + 1).start()
        return carry

    def tile_copy(turn, p):
        other = lax.rem(me + p, peers)
        return other, pltpu.make_async_remote_copy(
            src_ref=tiles.at[turn, me],
            dst_ref=tiles.at[turn, me],
            send_sem=tile_send.at[turn, p],
            recv_sem=tile_recv.at[turn, me],
            device_id=device(other // ops, lax.rem(other, ops)),
            device_id_type=MESH,
        )

    def send_sums(turn, rows):
        rows = list(rows) + [jnp.zeros((8 - len(rows), LANES), F32)]
        tiles[turn, me] = jnp.concatenate(rows, axis=0)

        def step(p, carry):
            tile_copy(turn, p)[1].start()
            return carry

        lax.fori_loop(1, peers, step, 0, unroll=peers <= 16)

    def take_sums(turn):
        def step(p, carry):
            other, copy = tile_copy(turn, p)
            pltpu.make_async_remote_copy(
                src_ref=tiles.at[turn, other],
                dst_ref=tiles.at[turn, other],
                send_sem=tile_send.at[turn, p],
                recv_sem=tile_recv.at[turn, other],
                device_id=device(other // ops, lax.rem(other, ops)),
                device_id_type=MESH,
            ).wait_recv()
            copy.wait_send()
            return carry

        lax.fori_loop(1, peers, step, 0, unroll=peers <= 16)
        total = jnp.sum(jnp.sum(tiles[turn], axis=0), axis=1, keepdims=True)
        return [total[i : i + 1, :] for i in range(8)]

    def vector_copy(j, d, o, source):
        return pltpu.make_async_remote_copy(
            src_ref=held[j].at[1, mine],
            dst_ref=held[j].at[d + 1, rows_of(source)],
            send_sem=v_send.at[j, d + 1, o],
            recv_sem=v_recv.at[j, d + 1, source],
            device_id=device(t + d, o),
            device_id_type=MESH,
        )

    def each_reader(action):
        for d in (1, -1, 0):
            def run(d=d):
                def step(p, carry):
                    action(d, lax.rem(q + p, ops))
                    return carry

                lax.fori_loop(1 if d == 0 else 0, ops, step, 0, unroll=True)

            if d == 0:
                run()
            else:
                pl.when((t + d >= 0) & (t + d < sectors))(run)

    def send_vector(j, values):
        held[j][1, mine] = values
        each_reader(lambda d, o: vector_copy(j, d, o, q).start())

    def take_vector(j):
        each_reader(lambda d, o: vector_copy(j, -d, o, o).wait_recv())
        each_reader(lambda d, o: vector_copy(j, d, o, q).wait_send())

    for j in range(3):
        @pl.when(t == 0)
        def _(j=j):
            held[j][2] = jnp.zeros((states, states), BF16)

        @pl.when(t == sectors - 1)
        def _(j=j):
            held[j][0] = jnp.zeros((states, states), BF16)

    for copy in small_copies:
        copy.wait()
    dims = dims_ref[0]
    row_at = lax.broadcasted_iota(jnp.int32, (quarter, states), 0) + q * quarter
    column_at = lax.broadcasted_iota(jnp.int32, (quarter, states), 1)
    mask = ((row_at < dims) & (column_at < dims)).astype(F32)
    onsite = onsite_ref[0, mine]

    masked = mask * wave_ref[0, mine].astype(F32)
    first_sums = [fold(masked * masked)]
    pl.semaphore_wait(barrier, peers - 1)
    send_sums(0, first_sums)
    early = min(2 * (sectors - 1), remote_blocks)
    lax.fori_loop(0, early, send_left, 0)
    start_norm = take_sums(0)[0]
    vector = (masked / jnp.sqrt(start_norm / entries + 1e-06)).astype(BF16)
    send_vector(0, vector)
    lax.fori_loop(early, remote_blocks, send_left, 0)
    right_copy.wait()
    own_copy.wait()

    def right_products(j):
        def step(i, carry):
            charge = charge_ref[(i // per * ops + q) * per + lax.rem(i, per)]
            pbuf[i] = lax.dot_general(
                held[j][charge + 1], rbuf[i], (((1,), (1,)), ((), ())),
                preferred_element_type=F32,
            ).astype(BF16)
            return carry

        lax.fori_loop(0, blocks, step, 0, unroll=4)

    def product(i):
        return jnp.dot(lbuf[i], pbuf[i], preferred_element_type=F32)

    group = 4 if blocks % 4 == 0 else 1

    def left_products(arriving):
        acc[...] = jnp.zeros_like(acc)
        if arriving:
            def own(k, carry):
                acc[...] += product(t * per + k)
                return carry

            lax.fori_loop(0, per, own, 0)

            def step(i, carry):
                at, copy = left_arrives(i // (sectors - 1), lax.rem(i, sectors - 1) + 1)
                copy.wait_recv()
                acc[...] += product(at)
                return carry

            lax.fori_loop(0, remote_blocks, step, 0)
        else:
            def step(i, carry):
                total = product(i * group)
                for n in range(1, group):
                    total = total + product(i * group + n)
                acc[...] += total
                return carry

            lax.fori_loop(0, blocks // group, step, 0)

    def part_copy(j, o, source):
        return pltpu.make_async_remote_copy(
            src_ref=part_send.at[j, rows_of(o)],
            dst_ref=part_recv.at[j, source],
            send_sem=part_send_sem.at[j, o],
            recv_sem=part_recv_sem.at[j, source],
            device_id=device(t, o),
            device_id_type=MESH,
        )

    def each_op(action):
        def step(p, carry):
            action(lax.rem(q + p, ops))
            return carry

        lax.fori_loop(1, ops, step, 0, unroll=True)

    def send_partial(j):
        part_send[j] = acc[...].astype(BF16)
        each_op(lambda o: part_copy(j, o, q).start())

    def take_partial(j, vector):
        part_recv[j, q] = part_send[j, mine]
        each_op(lambda o: part_copy(j, o, o).wait_recv())
        each_op(lambda o: part_copy(j, o, q).wait_send())
        total = acc[mine]
        own = part_recv[j, q].astype(F32)
        total = total + (jnp.sum(part_recv[j].astype(F32), axis=0) - own)
        return mask * (onsite * vector.astype(F32) + total)

    vectors = [vector]
    images = []
    norms = []
    ritz = []
    cross = []
    for j in range(3):
        current = vectors[j].astype(F32)
        take_vector(j)
        right_products(j)
        left_products(j == 0)
        send_partial(j)
        diagonal = onsite * current

        def overlap(i):
            whole = fold(held[i][1].astype(F32) * acc[...])
            return whole + fold(vectors[i].astype(F32) * diagonal)

        if j == 0:
            rows = [overlap(0), fold(current * current)]
        elif j == 1:
            first = vectors[0].astype(F32)
            rows = [
                overlap(1), fold(current * current), overlap(0),
                fold(current * images[0]), fold(first * current),
            ]
        else:
            rows = [
                overlap(2), overlap(0), overlap(1),
                fold(current * images[0]), fold(current * images[1]),
            ]
        send_sums(1 + 2 * j, rows)
        image = take_partial(j, vectors[j])
        images.append(image)
        if j == 2:
            break
        sums = take_sums(1 + 2 * j)
        ritz.append(sums)
        norms.append(sums[1])
        rayleigh = sums[0] / sums[1]
        correction = (image - rayleigh * current) / (1.0 + jnp.abs(onsite - rayleigh))
        send_sums(
            2 + 2 * j,
            [fold(correction * correction)]
            + [fold(older.astype(F32) * correction) for older in vectors],
        )
        seconds = take_sums(2 + 2 * j)
        length = seconds[0]
        update = correction
        factors = []
        for i in range(j + 1):
            factor = seconds[1 + i] / norms[i]
            factors.append(factor)
            update = update - factor * vectors[i].astype(F32)
            length = length - factor * seconds[1 + i]
        if j == 1:
            length = length + 2.0 * factors[0] * factors[1] * sums[4]
        length = jnp.maximum(length, 0.0)
        following = (update / jnp.sqrt(length / entries + 1e-06)).astype(BF16)
        vectors.append(following)
        send_vector(j + 1, following)

    full[mine] = images[2]

    def full_copy(o, source):
        return pltpu.make_async_remote_copy(
            src_ref=full.at[mine],
            dst_ref=full.at[rows_of(source)],
            send_sem=full_send.at[o],
            recv_sem=full_recv.at[source],
            device_id=device(t, o),
            device_id_type=MESH,
        )

    each_op(lambda o: full_copy(o, q).start())
    last = take_sums(5)
    values = [
        [ritz[0][0], ritz[1][2], last[1]],
        [ritz[1][3], ritz[1][0], last[2]],
        [last[3], last[4], last[0]],
    ]
    at_row = lax.broadcasted_iota(jnp.int32, (8, LANES), 0)
    at_column = lax.broadcasted_iota(jnp.int32, (8, LANES), 1)
    table = jnp.zeros((8, LANES), F32)
    for i in range(3):
        for n in range(3):
            table = jnp.where((at_row == i) & (at_column == n), values[i][n] / entries, table)
    corr_ref[...] = table[:3, :3]

    def sent_left(i, carry):
        left_copy(i // (sectors - 1), lax.rem(i, sectors - 1) + 1).wait_send()
        return carry

    lax.fori_loop(0, remote_blocks, sent_left, 0)
    each_op(lambda o: full_copy(o, o).wait_recv())
    each_op(lambda o: full_copy(o, q).wait_send())
    image_ref[0] = full[...]


def on_device(left_arrival, right_env, op_charge, sector_dims, wavefunction, onsite):
    sectors = lax.axis_size("sector")
    ops = lax.axis_size("op")
    per = left_arrival.shape[0]
    states = wavefunction.shape[1]
    blocks = sectors * per
    quarter = states // ops
    right = right_env.reshape(blocks, states, states)
    vmem = pl.BlockSpec(memory_space=pltpu.VMEM)
    anywhere = pl.BlockSpec(memory_space=pl.ANY)
    dma = pltpu.SemaphoreType.DMA
    return pl.pallas_call(
        functools.partial(davidson_kernel, sectors, ops),
        out_shape=(
            jax.ShapeDtypeStruct(wavefunction.shape, F32),
            jax.ShapeDtypeStruct((3, 3), F32),
        ),
        in_specs=[anywhere] * 6,
        out_specs=(vmem, vmem),
        scratch_shapes=[
            pltpu.SMEM(op_charge.shape, jnp.int32),
            pltpu.SMEM(sector_dims.shape, jnp.int32),
            pltpu.VMEM(wavefunction.shape, BF16),
            pltpu.VMEM(onsite.shape, F32),
            dma((4,)),
            pltpu.VMEM((blocks, states, states), BF16),
            pltpu.VMEM((blocks, states, states), BF16),
            pltpu.VMEM((blocks, states, states), BF16),
            pltpu.VMEM((states, states), F32),
            pltpu.VMEM((3, states, states), BF16),
            pltpu.VMEM((3, states, states), BF16),
            pltpu.VMEM((3, states, states), BF16),
            pltpu.VMEM((3, states, states), BF16),
            pltpu.VMEM((3, ops, quarter, states), BF16),
            pltpu.VMEM((states, states), F32),
            pltpu.VMEM((6, sectors * ops, 8, LANES), F32),
            dma,
            dma,
            dma((sectors, per)),
            dma((sectors, per)),
            dma((3, 3, ops)),
            dma((3, 3, ops)),
            dma((3, ops)),
            dma((3, ops)),
            dma((6, sectors * ops)),
            dma((6, sectors * ops)),
            dma((ops,)),
            dma((ops,)),
        ],
        compiler_params=pltpu.CompilerParams(
            collective_id=0, has_side_effects=True, vmem_limit_bytes=48 * 1024 * 1024
        ),
    )(left_arrival, right, op_charge, sector_dims, wavefunction, onsite)


def solution(mesh):
    in_specs = (
        P(("groups", "sector", "op"), None, None, None),
        P("groups", "op", None, "sector", None, None),
        P("groups"),
        P(("groups", "sector")),
        P(("groups", "sector"), None, None),
        P(("groups", "sector"), None, None),
    )
    out_specs = (P(("groups", "sector"), None, None), P("groups", None))
    return jax.shard_map(
        on_device, mesh=mesh, in_specs=in_specs, out_specs=out_specs, check_vma=False
    )
```

```python
import functools

import jax
import jax.numpy as jnp
from jax import lax
from jax.experimental import pallas as pl
from jax.experimental.pallas import tpu as pltpu
from jax.sharding import PartitionSpec as P

F32 = jnp.float32
BF16 = jnp.bfloat16
LANES = 128
MESH = pl.DeviceIdType.MESH


def fold(values):
    row = jnp.sum(values, axis=0, keepdims=True)
    total = row[:, :LANES]
    for start in range(LANES, row.shape[1], LANES):
        total = total + row[:, start : start + LANES]
    return total


def davidson_kernel(
    sectors, ops,
    left_ref, right_ref, charge_hbm, dims_hbm, wave_hbm, onsite_hbm,
    image_ref, corr_ref,
    charge_ref, dims_ref, wave_ref, onsite_ref, small_local, lbuf, rbuf, pbuf, acc, v0, v1, v2, part_send, part_recv, full, tiles,
    left_local, right_local, left_send, left_recv, v_send, v_recv,
    part_send_sem, part_recv_sem, tile_send, tile_recv, full_send, full_recv,
):
    held = (v0, v1, v2)
    t = lax.axis_index("sector")
    q = lax.axis_index("op")
    me = t * ops + q
    peers = sectors * ops
    per = left_ref.shape[0]
    states = wave_hbm.shape[1]
    quarter = states // ops
    blocks = sectors * per
    entries = sectors * states * states

    def rows_of(index):
        return pl.ds(pl.multiple_of(index * quarter, quarter), quarter)

    mine = rows_of(q)

    def device(s, o):
        return {"sector": s, "op": o}

    small_copies = [
        pltpu.make_async_copy(source, target, small_local.at[i])
        for i, (source, target) in enumerate((
            (dims_hbm, dims_ref), (wave_hbm, wave_ref), (onsite_hbm, onsite_ref),
            (charge_hbm, charge_ref),
        ))
    ]
    for copy in small_copies:
        copy.start()

    barrier = pltpu.get_barrier_semaphore()

    def greet(p, carry):
        other = lax.rem(me + p, peers)
        pl.semaphore_signal(
            barrier, inc=1, device_id=device(other // ops, lax.rem(other, ops)),
            device_id_type=MESH,
        )
        return carry

    lax.fori_loop(1, peers, greet, 0, unroll=peers <= 16)

    right_copy = pltpu.make_async_copy(right_ref, rbuf, right_local)
    right_copy.start()
    own_copy = pltpu.make_async_copy(
        left_ref.at[:, t], lbuf.at[pl.ds(t * per, per)], left_local
    )
    own_copy.start()

    def left_copy(k, p):
        target = lax.rem(t + p, sectors)
        return pltpu.make_async_remote_copy(
            src_ref=left_ref.at[k, target],
            dst_ref=lbuf.at[t * per + k],
            send_sem=left_send.at[p, k],
            recv_sem=left_recv.at[t, k],
            device_id=device(target, q),
            device_id_type=MESH,
        )

    def left_arrives(k, p):
        source = lax.rem(t + p, sectors)
        return source * per + k, pltpu.make_async_remote_copy(
            src_ref=left_ref.at[k, source],
            dst_ref=lbuf.at[source * per + k],
            send_sem=left_send.at[p, k],
            recv_sem=left_recv.at[source, k],
            device_id=device(source, q),
            device_id_type=MESH,
        )

    remote_blocks = per * (sectors - 1)

    def send_left(i, carry):
        left_copy(i // (sectors - 1), lax.rem(i, sectors - 1) + 1).start()
        return carry

    def tile_copy(turn, p):
        other = lax.rem(me + p, peers)
        return other, pltpu.make_async_remote_copy(
            src_ref=tiles.at[turn, me],
            dst_ref=tiles.at[turn, me],
            send_sem=tile_send.at[turn, p],
            recv_sem=tile_recv.at[turn, me],
            device_id=device(other // ops, lax.rem(other, ops)),
            device_id_type=MESH,
        )

    def send_sums(turn, rows):
        rows = list(rows) + [jnp.zeros((8 - len(rows), LANES), F32)]
        tiles[turn, me] = jnp.concatenate(rows, axis=0)

        def step(p, carry):
            tile_copy(turn, p)[1].start()
            return carry

        lax.fori_loop(1, peers, step, 0, unroll=peers <= 16)

    def take_sums(turn):
        def step(p, carry):
            other, copy = tile_copy(turn, p)
            pltpu.make_async_remote_copy(
                src_ref=tiles.at[turn, other],
                dst_ref=tiles.at[turn, other],
                send_sem=tile_send.at[turn, p],
                recv_sem=tile_recv.at[turn, other],
                device_id=device(other // ops, lax.rem(other, ops)),
                device_id_type=MESH,
            ).wait_recv()
            copy.wait_send()
            return carry

        lax.fori_loop(1, peers, step, 0, unroll=peers <= 16)
        total = jnp.sum(jnp.sum(tiles[turn], axis=0), axis=1, keepdims=True)
        return [total[i : i + 1, :] for i in range(8)]

    def vector_copy(j, d, o, source):
        return pltpu.make_async_remote_copy(
            src_ref=held[j].at[1, mine],
            dst_ref=held[j].at[d + 1, rows_of(source)],
            send_sem=v_send.at[j, d + 1, o],
            recv_sem=v_recv.at[j, d + 1, source],
            device_id=device(t + d, o),
            device_id_type=MESH,
        )

    def each_reader(action):
        for d in (1, -1, 0):
            def run(d=d):
                def step(p, carry):
                    action(d, lax.rem(q + p, ops))
                    return carry

                lax.fori_loop(1 if d == 0 else 0, ops, step, 0, unroll=True)

            if d == 0:
                run()
            else:
                pl.when((t + d >= 0) & (t + d < sectors))(run)

    def send_vector(j, values):
        held[j][1, mine] = values
        each_reader(lambda d, o: vector_copy(j, d, o, q).start())

    def take_vector(j):
        each_reader(lambda d, o: vector_copy(j, -d, o, o).wait_recv())
        each_reader(lambda d, o: vector_copy(j, d, o, q).wait_send())

    for j in range(3):
        @pl.when(t == 0)
        def _(j=j):
            held[j][2] = jnp.zeros((states, states), BF16)

        @pl.when(t == sectors - 1)
        def _(j=j):
            held[j][0] = jnp.zeros((states, states), BF16)

    for copy in small_copies:
        copy.wait()
    dims = dims_ref[0]
    row_at = lax.broadcasted_iota(jnp.int32, (quarter, states), 0) + q * quarter
    column_at = lax.broadcasted_iota(jnp.int32, (quarter, states), 1)
    mask = ((row_at < dims) & (column_at < dims)).astype(F32)
    onsite = onsite_ref[0, mine]

    masked = mask * wave_ref[0, mine].astype(F32)
    first_sums = [fold(masked * masked)]
    pl.semaphore_wait(barrier, peers - 1)
    send_sums(0, first_sums)
    early = min(2 * (sectors - 1), remote_blocks)
    lax.fori_loop(0, early, send_left, 0)
    start_norm = take_sums(0)[0]
    vector = (masked / jnp.sqrt(start_norm / entries + 1e-06)).astype(BF16)
    send_vector(0, vector)
    lax.fori_loop(early, remote_blocks, send_left, 0)
    right_copy.wait()
    own_copy.wait()

    def right_products(j):
        def step(i, carry):
            charge = charge_ref[(i // per * ops + q) * per + lax.rem(i, per)]
            pbuf[i] = lax.dot_general(
                held[j][charge + 1], rbuf[i], (((1,), (1,)), ((), ())),
                preferred_element_type=F32,
            ).astype(BF16)
            return carry

        lax.fori_loop(0, blocks, step, 0, unroll=8)

    def product(i):
        return jnp.dot(lbuf[i], pbuf[i], preferred_element_type=F32)

    group = max(n for n in (1, 2, 4, 8, 16, 32) if blocks % n == 0)

    def left_products(arriving):
        acc[...] = jnp.zeros_like(acc)
        if arriving:
            def own(k, carry):
                acc[...] += product(t * per + k)
                return carry

            lax.fori_loop(0, per, own, 0)

            def step(i, carry):
                at, copy = left_arrives(i // (sectors - 1), lax.rem(i, sectors - 1) + 1)
                copy.wait_recv()
                acc[...] += product(at)
                return carry

            lax.fori_loop(0, remote_blocks, step, 0)
        else:
            def step(i, carry):
                total = product(i * group)
                for n in range(1, group):
                    total = total + product(i * group + n)
                acc[...] += total
                return carry

            lax.fori_loop(0, blocks // group, step, 0)

    def part_copy(j, o, source):
        return pltpu.make_async_remote_copy(
            src_ref=part_send.at[j, rows_of(o)],
            dst_ref=part_recv.at[j, source],
            send_sem=part_send_sem.at[j, o],
            recv_sem=part_recv_sem.at[j, source],
            device_id=device(t, o),
            device_id_type=MESH,
        )

    def each_op(action):
        def step(p, carry):
            action(lax.rem(q + p, ops))
            return carry

        lax.fori_loop(1, ops, step, 0, unroll=True)

    def send_partial(j):
        part_send[j] = acc[...].astype(BF16)
        each_op(lambda o: part_copy(j, o, q).start())

    def take_partial(j, vector):
        part_recv[j, q] = part_send[j, mine]
        each_op(lambda o: part_copy(j, o, o).wait_recv())
        each_op(lambda o: part_copy(j, o, q).wait_send())
        total = acc[mine]
        own = part_recv[j, q].astype(F32)
        total = total + (jnp.sum(part_recv[j].astype(F32), axis=0) - own)
        return mask * (onsite * vector.astype(F32) + total)

    vectors = [vector]
    images = []
    norms = []
    ritz = []
    cross = []
    for j in range(3):
        current = vectors[j].astype(F32)
        take_vector(j)
        right_products(j)
        left_products(j == 0)
        send_partial(j)
        diagonal = onsite * current

        def overlap(i):
            whole = fold(held[i][1].astype(F32) * acc[...])
            return whole + fold(vectors[i].astype(F32) * diagonal)

        if j == 0:
            rows = [overlap(0), fold(current * current)]
        elif j == 1:
            first = vectors[0].astype(F32)
            rows = [
                overlap(1), fold(current * current), overlap(0),
                fold(current * images[0]), fold(first * current),
            ]
        else:
            rows = [
                overlap(2), overlap(0), overlap(1),
                fold(current * images[0]), fold(current * images[1]),
            ]
        send_sums(1 + 2 * j, rows)
        image = take_partial(j, vectors[j])
        images.append(image)
        if j == 2:
            break
        sums = take_sums(1 + 2 * j)
        ritz.append(sums)
        norms.append(sums[1])
        rayleigh = sums[0] / sums[1]
        correction = (image - rayleigh * current) / (1.0 + jnp.abs(onsite - rayleigh))
        send_sums(
            2 + 2 * j,
            [fold(correction * correction)]
            + [fold(older.astype(F32) * correction) for older in vectors],
        )
        seconds = take_sums(2 + 2 * j)
        length = seconds[0]
        update = correction
        factors = []
        for i in range(j + 1):
            factor = seconds[1 + i] / norms[i]
            factors.append(factor)
            update = update - factor * vectors[i].astype(F32)
            length = length - factor * seconds[1 + i]
        if j == 1:
            length = length + 2.0 * factors[0] * factors[1] * sums[4]
        length = jnp.maximum(length, 0.0)
        following = (update / jnp.sqrt(length / entries + 1e-06)).astype(BF16)
        vectors.append(following)
        send_vector(j + 1, following)

    full[mine] = images[2]

    def full_copy(o, source):
        return pltpu.make_async_remote_copy(
            src_ref=full.at[mine],
            dst_ref=full.at[rows_of(source)],
            send_sem=full_send.at[o],
            recv_sem=full_recv.at[source],
            device_id=device(t, o),
            device_id_type=MESH,
        )

    each_op(lambda o: full_copy(o, q).start())
    last = take_sums(5)
    values = [
        [ritz[0][0], ritz[1][2], last[1]],
        [ritz[1][3], ritz[1][0], last[2]],
        [last[3], last[4], last[0]],
    ]
    at_row = lax.broadcasted_iota(jnp.int32, (8, LANES), 0)
    at_column = lax.broadcasted_iota(jnp.int32, (8, LANES), 1)
    table = jnp.zeros((8, LANES), F32)
    for i in range(3):
        for n in range(3):
            table = jnp.where((at_row == i) & (at_column == n), values[i][n] / entries, table)
    corr_ref[...] = table[:3, :3]

    def sent_left(i, carry):
        left_copy(i // (sectors - 1), lax.rem(i, sectors - 1) + 1).wait_send()
        return carry

    lax.fori_loop(0, remote_blocks, sent_left, 0)
    each_op(lambda o: full_copy(o, o).wait_recv())
    each_op(lambda o: full_copy(o, q).wait_send())
    image_ref[0] = full[...]


def on_device(left_arrival, right_env, op_charge, sector_dims, wavefunction, onsite):
    sectors = lax.axis_size("sector")
    ops = lax.axis_size("op")
    per = left_arrival.shape[0]
    states = wavefunction.shape[1]
    blocks = sectors * per
    quarter = states // ops
    right = right_env.reshape(blocks, states, states)
    vmem = pl.BlockSpec(memory_space=pltpu.VMEM)
    anywhere = pl.BlockSpec(memory_space=pl.ANY)
    dma = pltpu.SemaphoreType.DMA
    return pl.pallas_call(
        functools.partial(davidson_kernel, sectors, ops),
        out_shape=(
            jax.ShapeDtypeStruct(wavefunction.shape, F32),
            jax.ShapeDtypeStruct((3, 3), F32),
        ),
        in_specs=[anywhere] * 6,
        out_specs=(vmem, vmem),
        scratch_shapes=[
            pltpu.SMEM(op_charge.shape, jnp.int32),
            pltpu.SMEM(sector_dims.shape, jnp.int32),
            pltpu.VMEM(wavefunction.shape, BF16),
            pltpu.VMEM(onsite.shape, F32),
            dma((4,)),
            pltpu.VMEM((blocks, states, states), BF16),
            pltpu.VMEM((blocks, states, states), BF16),
            pltpu.VMEM((blocks, states, states), BF16),
            pltpu.VMEM((states, states), F32),
            pltpu.VMEM((3, states, states), BF16),
            pltpu.VMEM((3, states, states), BF16),
            pltpu.VMEM((3, states, states), BF16),
            pltpu.VMEM((3, states, states), BF16),
            pltpu.VMEM((3, ops, quarter, states), BF16),
            pltpu.VMEM((states, states), F32),
            pltpu.VMEM((6, sectors * ops, 8, LANES), F32),
            dma,
            dma,
            dma((sectors, per)),
            dma((sectors, per)),
            dma((3, 3, ops)),
            dma((3, 3, ops)),
            dma((3, ops)),
            dma((3, ops)),
            dma((6, sectors * ops)),
            dma((6, sectors * ops)),
            dma((ops,)),
            dma((ops,)),
        ],
        compiler_params=pltpu.CompilerParams(
            collective_id=0, has_side_effects=True, vmem_limit_bytes=60 * 1024 * 1024
        ),
    )(left_arrival, right, op_charge, sector_dims, wavefunction, onsite)


def solution(mesh):
    in_specs = (
        P(("groups", "sector", "op"), None, None, None),
        P("groups", "op", None, "sector", None, None),
        P("groups"),
        P(("groups", "sector")),
        P(("groups", "sector"), None, None),
        P(("groups", "sector"), None, None),
    )
    out_specs = (P(("groups", "sector"), None, None), P("groups", None))
    return jax.shard_map(
        on_device, mesh=mesh, in_specs=in_specs, out_specs=out_specs, check_vma=False
    )
```

```python
import functools

import jax
import jax.numpy as jnp
from jax import lax
from jax.experimental import pallas as pl
from jax.experimental.pallas import tpu as pltpu
from jax.sharding import PartitionSpec as P

F32 = jnp.float32
BF16 = jnp.bfloat16
LANES = 128
MESH = pl.DeviceIdType.MESH


def fold(values):
    row = jnp.sum(values, axis=0, keepdims=True)
    total = row[:, :LANES]
    for start in range(LANES, row.shape[1], LANES):
        total = total + row[:, start : start + LANES]
    return total


def davidson_kernel(
    sectors, ops,
    left_ref, right_ref, charge_hbm, dims_hbm, wave_hbm, onsite_hbm,
    image_ref, corr_ref,
    charge_ref, dims_ref, wave_ref, onsite_ref, small_local, lbuf, rbuf, pbuf, acc, v0, v1, v2, part_send, part_recv, full, tiles,
    left_local, right_local, left_send, left_recv, v_send, v_recv,
    part_send_sem, part_recv_sem, tile_send, tile_recv, full_send, full_recv,
):
    held = (v0, v1, v2)
    t = lax.axis_index("sector")
    q = lax.axis_index("op")
    me = t * ops + q
    peers = sectors * ops
    per = left_ref.shape[0]
    states = wave_hbm.shape[1]
    quarter = states // ops
    blocks = sectors * per
    entries = sectors * states * states

    def rows_of(index):
        return pl.ds(pl.multiple_of(index * quarter, quarter), quarter)

    mine = rows_of(q)

    def device(s, o):
        return {"sector": s, "op": o}

    small_copies = [
        pltpu.make_async_copy(source, target, small_local.at[i])
        for i, (source, target) in enumerate((
            (dims_hbm, dims_ref), (wave_hbm, wave_ref), (onsite_hbm, onsite_ref),
            (charge_hbm, charge_ref),
        ))
    ]
    for copy in small_copies:
        copy.start()

    barrier = pltpu.get_barrier_semaphore()

    def greet(p, carry):
        other = lax.rem(me + p, peers)
        pl.semaphore_signal(
            barrier, inc=1, device_id=device(other // ops, lax.rem(other, ops)),
            device_id_type=MESH,
        )
        return carry

    lax.fori_loop(1, peers, greet, 0, unroll=peers <= 16)

    right_copy = pltpu.make_async_copy(right_ref, rbuf, right_local)
    right_copy.start()
    own_copy = pltpu.make_async_copy(
        left_ref.at[:, t], lbuf.at[pl.ds(t * per, per)], left_local
    )
    own_copy.start()

    def left_copy(k, p):
        target = lax.rem(t + p, sectors)
        return pltpu.make_async_remote_copy(
            src_ref=left_ref.at[k, target],
            dst_ref=lbuf.at[t * per + k],
            send_sem=left_send.at[p, k],
            recv_sem=left_recv.at[t, k],
            device_id=device(target, q),
            device_id_type=MESH,
        )

    def left_arrives(k, p):
        source = lax.rem(t + p, sectors)
        return source * per + k, pltpu.make_async_remote_copy(
            src_ref=left_ref.at[k, source],
            dst_ref=lbuf.at[source * per + k],
            send_sem=left_send.at[p, k],
            recv_sem=left_recv.at[source, k],
            device_id=device(source, q),
            device_id_type=MESH,
        )

    remote_blocks = per * (sectors - 1)

    def send_left(i, carry):
        left_copy(i // (sectors - 1), lax.rem(i, sectors - 1) + 1).start()
        return carry

    def tile_copy(turn, p):
        other = lax.rem(me + p, peers)
        return other, pltpu.make_async_remote_copy(
            src_ref=tiles.at[turn, me],
            dst_ref=tiles.at[turn, me],
            send_sem=tile_send.at[turn, p],
            recv_sem=tile_recv.at[turn, me],
            device_id=device(other // ops, lax.rem(other, ops)),
            device_id_type=MESH,
        )

    def send_sums(turn, rows):
        rows = list(rows) + [jnp.zeros((8 - len(rows), LANES), F32)]
        tiles[turn, me] = jnp.concatenate(rows, axis=0)

        def step(p, carry):
            tile_copy(turn, p)[1].start()
            return carry

        lax.fori_loop(1, peers, step, 0, unroll=peers <= 16)

    def take_sums(turn):
        def step(p, carry):
            other, copy = tile_copy(turn, p)
            pltpu.make_async_remote_copy(
                src_ref=tiles.at[turn, other],
                dst_ref=tiles.at[turn, other],
                send_sem=tile_send.at[turn, p],
                recv_sem=tile_recv.at[turn, other],
                device_id=device(other // ops, lax.rem(other, ops)),
                device_id_type=MESH,
            ).wait_recv()
            copy.wait_send()
            return carry

        lax.fori_loop(1, peers, step, 0, unroll=peers <= 16)
        total = jnp.sum(jnp.sum(tiles[turn], axis=0), axis=1, keepdims=True)
        return [total[i : i + 1, :] for i in range(8)]

    def vector_copy(j, d, o, source):
        return pltpu.make_async_remote_copy(
            src_ref=held[j].at[1, mine],
            dst_ref=held[j].at[d + 1, rows_of(source)],
            send_sem=v_send.at[j, d + 1, o],
            recv_sem=v_recv.at[j, d + 1, source],
            device_id=device(t + d, o),
            device_id_type=MESH,
        )

    def each_reader(action):
        for d in (1, -1, 0):
            def run(d=d):
                def step(p, carry):
                    action(d, lax.rem(q + p, ops))
                    return carry

                lax.fori_loop(1 if d == 0 else 0, ops, step, 0, unroll=True)

            if d == 0:
                run()
            else:
                pl.when((t + d >= 0) & (t + d < sectors))(run)

    def each_op(action):
        def step(p, carry):
            action(lax.rem(q + p, ops))
            return carry

        lax.fori_loop(1, ops, step, 0, unroll=True)

    def send_vector(j, values):
        held[j][1, mine] = values
        each_reader(lambda d, o: vector_copy(j, d, o, q).start())

    def take_vector(j):
        each_reader(lambda d, o: vector_copy(j, -d, o, o).wait_recv())
        each_reader(lambda d, o: vector_copy(j, d, o, q).wait_send())

    for j in range(3):
        @pl.when(t == 0)
        def _(j=j):
            held[j][2] = jnp.zeros((states, states), BF16)

        @pl.when(t == sectors - 1)
        def _(j=j):
            held[j][0] = jnp.zeros((states, states), BF16)

    for copy in small_copies:
        copy.wait()
    dims = dims_ref[0]
    row_at = lax.broadcasted_iota(jnp.int32, (quarter, states), 0) + q * quarter
    column_at = lax.broadcasted_iota(jnp.int32, (quarter, states), 1)
    mask = ((row_at < dims) & (column_at < dims)).astype(F32)
    onsite = onsite_ref[0, mine]

    masked = mask * wave_ref[0, mine].astype(F32)
    first_sums = [fold(masked * masked)]
    pl.semaphore_wait(barrier, peers - 1)
    send_sums(0, first_sums)
    early = min(2 * (sectors - 1), remote_blocks)
    lax.fori_loop(0, early, send_left, 0)
    start_norm = take_sums(0)[0]
    vector = (masked / jnp.sqrt(start_norm / entries + 1e-06)).astype(BF16)
    def relay_copy(d, o, source):
        return pltpu.make_async_remote_copy(
            src_ref=v0.at[d + 1, rows_of(source)],
            dst_ref=v0.at[d + 1, rows_of(source)],
            send_sem=v_send.at[0, d + 1, o],
            recv_sem=v_recv.at[0, d + 1, source],
            device_id=device(t, o),
            device_id_type=MESH,
        )

    def present(d):
        return (t + d >= 0) & (t + d < sectors)

    v0[1, mine] = vector
    for d in (1, -1):
        @pl.when(present(d))
        def _(d=d):
            vector_copy(0, d, q, q).start()
    each_op(lambda o: relay_copy(0, o, q).start())
    lax.fori_loop(early, remote_blocks, send_left, 0)
    for d in (1, -1):
        @pl.when(present(-d))
        def _(d=d):
            vector_copy(0, d, q, q).wait_recv()
            each_op(lambda o: relay_copy(d, o, q).start())
    each_op(lambda o: relay_copy(0, o, o).wait_recv())
    for d in (1, -1):
        @pl.when(present(-d))
        def _(d=d):
            each_op(lambda o: relay_copy(d, o, o).wait_recv())
            each_op(lambda o: relay_copy(d, o, q).wait_send())

        @pl.when(present(d))
        def _(d=d):
            vector_copy(0, d, q, q).wait_send()
    each_op(lambda o: relay_copy(0, o, q).wait_send())
    right_copy.wait()
    own_copy.wait()

    def right_products(j):
        def step(i, carry):
            charge = charge_ref[(i // per * ops + q) * per + lax.rem(i, per)]
            pbuf[i] = lax.dot_general(
                held[j][charge + 1], rbuf[i], (((1,), (1,)), ((), ())),
                preferred_element_type=F32,
            ).astype(BF16)
            return carry

        lax.fori_loop(0, blocks, step, 0, unroll=8)

    def product(i):
        return jnp.dot(lbuf[i], pbuf[i], preferred_element_type=F32)

    group = max(n for n in (1, 2, 4, 8, 16, 32) if blocks % n == 0)

    def left_products(arriving):
        acc[...] = jnp.zeros_like(acc)
        if arriving:
            def own(k, carry):
                acc[...] += product(t * per + k)
                return carry

            lax.fori_loop(0, per, own, 0)

            def step(i, carry):
                at, copy = left_arrives(i // (sectors - 1), lax.rem(i, sectors - 1) + 1)
                copy.wait_recv()
                acc[...] += product(at)
                return carry

            lax.fori_loop(0, remote_blocks, step, 0)
        else:
            def step(i, carry):
                total = product(i * group)
                for n in range(1, group):
                    total = total + product(i * group + n)
                acc[...] += total
                return carry

            lax.fori_loop(0, blocks // group, step, 0)

    def part_copy(j, o, source):
        return pltpu.make_async_remote_copy(
            src_ref=part_send.at[j, rows_of(o)],
            dst_ref=part_recv.at[j, source],
            send_sem=part_send_sem.at[j, o],
            recv_sem=part_recv_sem.at[j, source],
            device_id=device(t, o),
            device_id_type=MESH,
        )

    def send_partial(j):
        part_send[j] = acc[...].astype(BF16)
        each_op(lambda o: part_copy(j, o, q).start())

    def take_partial(j, vector):
        part_recv[j, q] = part_send[j, mine]
        each_op(lambda o: part_copy(j, o, o).wait_recv())
        each_op(lambda o: part_copy(j, o, q).wait_send())
        total = acc[mine]
        own = part_recv[j, q].astype(F32)
        total = total + (jnp.sum(part_recv[j].astype(F32), axis=0) - own)
        return mask * (onsite * vector.astype(F32) + total)

    vectors = [vector]
    images = []
    norms = []
    ritz = []
    cross = []
    for j in range(3):
        current = vectors[j].astype(F32)
        if j > 0:
            take_vector(j)
        right_products(j)
        left_products(j == 0)
        send_partial(j)
        diagonal = onsite * current

        def overlap(i):
            whole = fold(held[i][1].astype(F32) * acc[...])
            return whole + fold(vectors[i].astype(F32) * diagonal)

        if j == 0:
            rows = [overlap(0), fold(current * current)]
        elif j == 1:
            first = vectors[0].astype(F32)
            rows = [
                overlap(1), fold(current * current), overlap(0),
                fold(current * images[0]), fold(first * current),
            ]
        else:
            rows = [
                overlap(2), overlap(0), overlap(1),
                fold(current * images[0]), fold(current * images[1]),
            ]
        send_sums(1 + 2 * j, rows)
        image = take_partial(j, vectors[j])
        images.append(image)
        if j == 2:
            break
        sums = take_sums(1 + 2 * j)
        ritz.append(sums)
        norms.append(sums[1])
        rayleigh = sums[0] / sums[1]
        correction = (image - rayleigh * current) / (1.0 + jnp.abs(onsite - rayleigh))
        send_sums(
            2 + 2 * j,
            [fold(correction * correction)]
            + [fold(older.astype(F32) * correction) for older in vectors],
        )
        seconds = take_sums(2 + 2 * j)
        length = seconds[0]
        update = correction
        factors = []
        for i in range(j + 1):
            factor = seconds[1 + i] / norms[i]
            factors.append(factor)
            update = update - factor * vectors[i].astype(F32)
            length = length - factor * seconds[1 + i]
        if j == 1:
            length = length + 2.0 * factors[0] * factors[1] * sums[4]
        length = jnp.maximum(length, 0.0)
        following = (update / jnp.sqrt(length / entries + 1e-06)).astype(BF16)
        vectors.append(following)
        send_vector(j + 1, following)

    full[mine] = images[2]

    def full_copy(o, source):
        return pltpu.make_async_remote_copy(
            src_ref=full.at[mine],
            dst_ref=full.at[rows_of(source)],
            send_sem=full_send.at[o],
            recv_sem=full_recv.at[source],
            device_id=device(t, o),
            device_id_type=MESH,
        )

    each_op(lambda o: full_copy(o, q).start())
    last = take_sums(5)
    values = [
        [ritz[0][0], ritz[1][2], last[1]],
        [ritz[1][3], ritz[1][0], last[2]],
        [last[3], last[4], last[0]],
    ]
    at_row = lax.broadcasted_iota(jnp.int32, (8, LANES), 0)
    at_column = lax.broadcasted_iota(jnp.int32, (8, LANES), 1)
    table = jnp.zeros((8, LANES), F32)
    for i in range(3):
        for n in range(3):
            table = jnp.where((at_row == i) & (at_column == n), values[i][n] / entries, table)
    corr_ref[...] = table[:3, :3]

    def sent_left(i, carry):
        left_copy(i // (sectors - 1), lax.rem(i, sectors - 1) + 1).wait_send()
        return carry

    lax.fori_loop(0, remote_blocks, sent_left, 0)
    each_op(lambda o: full_copy(o, o).wait_recv())
    each_op(lambda o: full_copy(o, q).wait_send())
    image_ref[0] = full[...]


def on_device(left_arrival, right_env, op_charge, sector_dims, wavefunction, onsite):
    sectors = lax.axis_size("sector")
    ops = lax.axis_size("op")
    per = left_arrival.shape[0]
    states = wavefunction.shape[1]
    blocks = sectors * per
    quarter = states // ops
    right = right_env.reshape(blocks, states, states)
    vmem = pl.BlockSpec(memory_space=pltpu.VMEM)
    anywhere = pl.BlockSpec(memory_space=pl.ANY)
    dma = pltpu.SemaphoreType.DMA
    return pl.pallas_call(
        functools.partial(davidson_kernel, sectors, ops),
        out_shape=(
            jax.ShapeDtypeStruct(wavefunction.shape, F32),
            jax.ShapeDtypeStruct((3, 3), F32),
        ),
        in_specs=[anywhere] * 6,
        out_specs=(vmem, vmem),
        scratch_shapes=[
            pltpu.SMEM(op_charge.shape, jnp.int32),
            pltpu.SMEM(sector_dims.shape, jnp.int32),
            pltpu.VMEM(wavefunction.shape, BF16),
            pltpu.VMEM(onsite.shape, F32),
            dma((4,)),
            pltpu.VMEM((blocks, states, states), BF16),
            pltpu.VMEM((blocks, states, states), BF16),
            pltpu.VMEM((blocks, states, states), BF16),
            pltpu.VMEM((states, states), F32),
            pltpu.VMEM((3, states, states), BF16),
            pltpu.VMEM((3, states, states), BF16),
            pltpu.VMEM((3, states, states), BF16),
            pltpu.VMEM((3, states, states), BF16),
            pltpu.VMEM((3, ops, quarter, states), BF16),
            pltpu.VMEM((states, states), F32),
            pltpu.VMEM((6, sectors * ops, 8, LANES), F32),
            dma,
            dma,
            dma((sectors, per)),
            dma((sectors, per)),
            dma((3, 3, ops)),
            dma((3, 3, ops)),
            dma((3, ops)),
            dma((3, ops)),
            dma((6, sectors * ops)),
            dma((6, sectors * ops)),
            dma((ops,)),
            dma((ops,)),
        ],
        compiler_params=pltpu.CompilerParams(
            collective_id=0, has_side_effects=True, vmem_limit_bytes=60 * 1024 * 1024
        ),
    )(left_arrival, right, op_charge, sector_dims, wavefunction, onsite)


def solution(mesh):
    in_specs = (
        P(("groups", "sector", "op"), None, None, None),
        P("groups", "op", None, "sector", None, None),
        P("groups"),
        P(("groups", "sector")),
        P(("groups", "sector"), None, None),
        P(("groups", "sector"), None, None),
    )
    out_specs = (P(("groups", "sector"), None, None), P("groups", None))
    return jax.shard_map(
        on_device, mesh=mesh, in_specs=in_specs, out_specs=out_specs, check_vma=False
    )
```

```python
import functools

import jax
import jax.numpy as jnp
from jax import lax
from jax.experimental import pallas as pl
from jax.experimental.pallas import tpu as pltpu
from jax.sharding import PartitionSpec as P

F32 = jnp.float32
BF16 = jnp.bfloat16
LANES = 128
MESH = pl.DeviceIdType.MESH


def fold(values):
    row = jnp.sum(values, axis=0, keepdims=True)
    total = row[:, :LANES]
    for start in range(LANES, row.shape[1], LANES):
        total = total + row[:, start : start + LANES]
    return total


def davidson_kernel(
    sectors, ops,
    left_ref, right_ref, charge_hbm, dims_hbm, wave_hbm, onsite_hbm,
    image_ref, corr_ref,
    charge_ref, dims_ref, wave_ref, onsite_ref, small_local, lbuf, rbuf, pbuf, acc, v0, v1, v2, part_send, part_recv, full, tiles,
    left_local, right_local, left_send, left_recv, v_send, v_recv,
    part_send_sem, part_recv_sem, tile_send, tile_recv, full_send, full_recv,
):
    held = (v0, v1, v2)
    t = lax.axis_index("sector")
    q = lax.axis_index("op")
    me = t * ops + q
    peers = sectors * ops
    per = left_ref.shape[0]
    states = wave_hbm.shape[1]
    quarter = states // ops
    blocks = sectors * per
    entries = sectors * states * states

    def rows_of(index):
        return pl.ds(pl.multiple_of(index * quarter, quarter), quarter)

    mine = rows_of(q)

    def device(s, o):
        return {"sector": s, "op": o}

    small_copies = [
        pltpu.make_async_copy(source, target, small_local.at[i])
        for i, (source, target) in enumerate((
            (dims_hbm, dims_ref), (wave_hbm, wave_ref), (onsite_hbm, onsite_ref),
            (charge_hbm, charge_ref),
        ))
    ]
    for copy in small_copies:
        copy.start()

    barrier = pltpu.get_barrier_semaphore()

    def greet(p, carry):
        other = lax.rem(me + p, peers)
        pl.semaphore_signal(
            barrier, inc=1, device_id=device(other // ops, lax.rem(other, ops)),
            device_id_type=MESH,
        )
        return carry

    lax.fori_loop(1, peers, greet, 0, unroll=peers <= 16)

    right_copy = pltpu.make_async_copy(right_ref, rbuf, right_local)
    right_copy.start()
    own_copy = pltpu.make_async_copy(
        left_ref.at[:, t], lbuf.at[pl.ds(t * per, per)], left_local
    )
    own_copy.start()

    def left_copy(k, p):
        target = lax.rem(t + p, sectors)
        return pltpu.make_async_remote_copy(
            src_ref=left_ref.at[k, target],
            dst_ref=lbuf.at[t * per + k],
            send_sem=left_send.at[p, k],
            recv_sem=left_recv.at[t, k],
            device_id=device(target, q),
            device_id_type=MESH,
        )

    def left_arrives(k, p):
        source = lax.rem(t + p, sectors)
        return source * per + k, pltpu.make_async_remote_copy(
            src_ref=left_ref.at[k, source],
            dst_ref=lbuf.at[source * per + k],
            send_sem=left_send.at[p, k],
            recv_sem=left_recv.at[source, k],
            device_id=device(source, q),
            device_id_type=MESH,
        )

    remote_blocks = per * (sectors - 1)

    def send_left(i, carry):
        left_copy(i // (sectors - 1), lax.rem(i, sectors - 1) + 1).start()
        return carry

    def tile_copy(turn, p):
        other = lax.rem(me + p, peers)
        return other, pltpu.make_async_remote_copy(
            src_ref=tiles.at[turn, me],
            dst_ref=tiles.at[turn, me],
            send_sem=tile_send.at[turn, p],
            recv_sem=tile_recv.at[turn, me],
            device_id=device(other // ops, lax.rem(other, ops)),
            device_id_type=MESH,
        )

    def send_sums(turn, rows):
        rows = list(rows) + [jnp.zeros((8 - len(rows), LANES), F32)]
        tiles[turn, me] = jnp.concatenate(rows, axis=0)

        def step(p, carry):
            tile_copy(turn, p)[1].start()
            return carry

        lax.fori_loop(1, peers, step, 0, unroll=peers <= 16)

    def take_sums(turn):
        def step(p, carry):
            other, copy = tile_copy(turn, p)
            pltpu.make_async_remote_copy(
                src_ref=tiles.at[turn, other],
                dst_ref=tiles.at[turn, other],
                send_sem=tile_send.at[turn, p],
                recv_sem=tile_recv.at[turn, other],
                device_id=device(other // ops, lax.rem(other, ops)),
                device_id_type=MESH,
            ).wait_recv()
            copy.wait_send()
            return carry

        lax.fori_loop(1, peers, step, 0, unroll=peers <= 16)
        total = jnp.sum(jnp.sum(tiles[turn], axis=0), axis=1, keepdims=True)
        return [total[i : i + 1, :] for i in range(8)]

    def vector_copy(j, d, o, source):
        return pltpu.make_async_remote_copy(
            src_ref=held[j].at[1, mine],
            dst_ref=held[j].at[d + 1, rows_of(source)],
            send_sem=v_send.at[j, d + 1, o],
            recv_sem=v_recv.at[j, d + 1, source],
            device_id=device(t + d, o),
            device_id_type=MESH,
        )

    def each_reader(action):
        for d in (1, -1, 0):
            def run(d=d):
                def step(p, carry):
                    action(d, lax.rem(q + p, ops))
                    return carry

                lax.fori_loop(1 if d == 0 else 0, ops, step, 0, unroll=True)

            if d == 0:
                run()
            else:
                pl.when((t + d >= 0) & (t + d < sectors))(run)

    def each_op(action):
        def step(p, carry):
            action(lax.rem(q + p, ops))
            return carry

        lax.fori_loop(1, ops, step, 0, unroll=True)

    def send_vector(j, values):
        held[j][1, mine] = values
        each_reader(lambda d, o: vector_copy(j, d, o, q).start())

    def take_vector(j):
        each_reader(lambda d, o: vector_copy(j, -d, o, o).wait_recv())
        each_reader(lambda d, o: vector_copy(j, d, o, q).wait_send())

    for j in range(3):
        @pl.when(t == 0)
        def _(j=j):
            held[j][2] = jnp.zeros((states, states), BF16)

        @pl.when(t == sectors - 1)
        def _(j=j):
            held[j][0] = jnp.zeros((states, states), BF16)

    for copy in small_copies:
        copy.wait()
    dims = dims_ref[0]
    row_at = lax.broadcasted_iota(jnp.int32, (quarter, states), 0) + q * quarter
    column_at = lax.broadcasted_iota(jnp.int32, (quarter, states), 1)
    mask = ((row_at < dims) & (column_at < dims)).astype(F32)
    onsite = onsite_ref[0, mine]

    masked = mask * wave_ref[0, mine].astype(F32)
    first_sums = [fold(masked * masked)]
    pl.semaphore_wait(barrier, peers - 1)
    send_sums(0, first_sums)
    early = min(2 * (sectors - 1), remote_blocks)
    lax.fori_loop(0, early, send_left, 0)
    start_norm = take_sums(0)[0]
    vector = (masked / jnp.sqrt(start_norm / entries + 1e-06)).astype(BF16)
    def relay_copy(d, o, source):
        return pltpu.make_async_remote_copy(
            src_ref=v0.at[d + 1, rows_of(source)],
            dst_ref=v0.at[d + 1, rows_of(source)],
            send_sem=v_send.at[0, d + 1, o],
            recv_sem=v_recv.at[0, d + 1, source],
            device_id=device(t, o),
            device_id_type=MESH,
        )

    def present(d):
        return (t + d >= 0) & (t + d < sectors)

    v0[1, mine] = vector
    for d in (1, -1):
        @pl.when(present(d))
        def _(d=d):
            vector_copy(0, d, q, q).start()
    each_op(lambda o: relay_copy(0, o, q).start())
    lax.fori_loop(early, remote_blocks, send_left, 0)
    for d in (1, -1):
        @pl.when(present(-d))
        def _(d=d):
            vector_copy(0, d, q, q).wait_recv()
            each_op(lambda o: relay_copy(d, o, q).start())
    each_op(lambda o: relay_copy(0, o, o).wait_recv())
    for d in (1, -1):
        @pl.when(present(-d))
        def _(d=d):
            each_op(lambda o: relay_copy(d, o, o).wait_recv())
            each_op(lambda o: relay_copy(d, o, q).wait_send())

        @pl.when(present(d))
        def _(d=d):
            vector_copy(0, d, q, q).wait_send()
    each_op(lambda o: relay_copy(0, o, q).wait_send())
    right_copy.wait()
    own_copy.wait()

    def right_products(j):
        def step(i, carry):
            charge = charge_ref[(i // per * ops + q) * per + lax.rem(i, per)]
            pbuf[i] = lax.dot_general(
                held[j][charge + 1], rbuf[i], (((1,), (1,)), ((), ())),
                preferred_element_type=F32,
            ).astype(BF16)
            return carry

        lax.fori_loop(0, blocks, step, 0, unroll=16)

    def product(i):
        return jnp.dot(lbuf[i], pbuf[i], preferred_element_type=F32)

    group = max(n for n in (1, 2, 4, 8, 16, 32) if blocks % n == 0)

    def left_products(arriving):
        acc[...] = jnp.zeros_like(acc)
        if arriving:
            def own(k, carry):
                acc[...] += product(t * per + k)
                return carry

            lax.fori_loop(0, per, own, 0)

            def step(i, carry):
                at, copy = left_arrives(i // (sectors - 1), lax.rem(i, sectors - 1) + 1)
                copy.wait_recv()
                acc[...] += product(at)
                return carry

            lax.fori_loop(0, remote_blocks, step, 0)
        else:
            def step(i, carry):
                total = product(i * group)
                for n in range(1, group):
                    total = total + product(i * group + n)
                acc[...] += total
                return carry

            lax.fori_loop(0, blocks // group, step, 0)

    def part_copy(j, o, source):
        return pltpu.make_async_remote_copy(
            src_ref=part_send.at[j, rows_of(o)],
            dst_ref=part_recv.at[j, source],
            send_sem=part_send_sem.at[j, o],
            recv_sem=part_recv_sem.at[j, source],
            device_id=device(t, o),
            device_id_type=MESH,
        )

    def send_partial(j):
        part_send[j] = acc[...].astype(BF16)
        each_op(lambda o: part_copy(j, o, q).start())

    def take_partial(j, vector):
        part_recv[j, q] = part_send[j, mine]
        each_op(lambda o: part_copy(j, o, o).wait_recv())
        each_op(lambda o: part_copy(j, o, q).wait_send())
        total = acc[mine]
        own = part_recv[j, q].astype(F32)
        total = total + (jnp.sum(part_recv[j].astype(F32), axis=0) - own)
        return mask * (onsite * vector.astype(F32) + total)

    vectors = [vector]
    images = []
    norms = []
    ritz = []
    cross = []
    for j in range(3):
        current = vectors[j].astype(F32)
        if j > 0:
            take_vector(j)
        right_products(j)
        left_products(j == 0)
        send_partial(j)
        diagonal = onsite * current

        def overlap(i):
            whole = fold(held[i][1].astype(F32) * acc[...])
            return whole + fold(vectors[i].astype(F32) * diagonal)

        if j == 0:
            rows = [overlap(0), fold(current * current)]
        elif j == 1:
            first = vectors[0].astype(F32)
            rows = [
                overlap(1), fold(current * current), overlap(0),
                fold(current * images[0]), fold(first * current),
            ]
        else:
            rows = [
                overlap(2), overlap(0), overlap(1),
                fold(current * images[0]), fold(current * images[1]),
            ]
        send_sums(1 + 2 * j, rows)
        image = take_partial(j, vectors[j])
        images.append(image)
        if j == 2:
            break
        sums = take_sums(1 + 2 * j)
        ritz.append(sums)
        norms.append(sums[1])
        rayleigh = sums[0] / sums[1]
        correction = (image - rayleigh * current) / (1.0 + jnp.abs(onsite - rayleigh))
        send_sums(
            2 + 2 * j,
            [fold(correction * correction)]
            + [fold(older.astype(F32) * correction) for older in vectors],
        )
        seconds = take_sums(2 + 2 * j)
        length = seconds[0]
        update = correction
        factors = []
        for i in range(j + 1):
            factor = seconds[1 + i] / norms[i]
            factors.append(factor)
            update = update - factor * vectors[i].astype(F32)
            length = length - factor * seconds[1 + i]
        if j == 1:
            length = length + 2.0 * factors[0] * factors[1] * sums[4]
        length = jnp.maximum(length, 0.0)
        following = (update / jnp.sqrt(length / entries + 1e-06)).astype(BF16)
        vectors.append(following)
        send_vector(j + 1, following)

    full[mine] = images[2]

    def full_copy(o, source):
        return pltpu.make_async_remote_copy(
            src_ref=full.at[mine],
            dst_ref=full.at[rows_of(source)],
            send_sem=full_send.at[o],
            recv_sem=full_recv.at[source],
            device_id=device(t, o),
            device_id_type=MESH,
        )

    each_op(lambda o: full_copy(o, q).start())
    last = take_sums(5)
    values = [
        [ritz[0][0], ritz[1][2], last[1]],
        [ritz[1][3], ritz[1][0], last[2]],
        [last[3], last[4], last[0]],
    ]
    at_row = lax.broadcasted_iota(jnp.int32, (8, LANES), 0)
    at_column = lax.broadcasted_iota(jnp.int32, (8, LANES), 1)
    table = jnp.zeros((8, LANES), F32)
    for i in range(3):
        for n in range(3):
            table = jnp.where((at_row == i) & (at_column == n), values[i][n] / entries, table)
    corr_ref[...] = table[:3, :3]

    def sent_left(i, carry):
        left_copy(i // (sectors - 1), lax.rem(i, sectors - 1) + 1).wait_send()
        return carry

    lax.fori_loop(0, remote_blocks, sent_left, 0)
    each_op(lambda o: full_copy(o, o).wait_recv())
    each_op(lambda o: full_copy(o, q).wait_send())
    image_ref[0] = full[...]


def on_device(left_arrival, right_env, op_charge, sector_dims, wavefunction, onsite):
    sectors = lax.axis_size("sector")
    ops = lax.axis_size("op")
    per = left_arrival.shape[0]
    states = wavefunction.shape[1]
    blocks = sectors * per
    quarter = states // ops
    right = right_env.reshape(blocks, states, states)
    vmem = pl.BlockSpec(memory_space=pltpu.VMEM)
    anywhere = pl.BlockSpec(memory_space=pl.ANY)
    dma = pltpu.SemaphoreType.DMA
    return pl.pallas_call(
        functools.partial(davidson_kernel, sectors, ops),
        out_shape=(
            jax.ShapeDtypeStruct(wavefunction.shape, F32),
            jax.ShapeDtypeStruct((3, 3), F32),
        ),
        in_specs=[anywhere] * 6,
        out_specs=(vmem, vmem),
        scratch_shapes=[
            pltpu.SMEM(op_charge.shape, jnp.int32),
            pltpu.SMEM(sector_dims.shape, jnp.int32),
            pltpu.VMEM(wavefunction.shape, BF16),
            pltpu.VMEM(onsite.shape, F32),
            dma((4,)),
            pltpu.VMEM((blocks, states, states), BF16),
            pltpu.VMEM((blocks, states, states), BF16),
            pltpu.VMEM((blocks, states, states), BF16),
            pltpu.VMEM((states, states), F32),
            pltpu.VMEM((3, states, states), BF16),
            pltpu.VMEM((3, states, states), BF16),
            pltpu.VMEM((3, states, states), BF16),
            pltpu.VMEM((3, states, states), BF16),
            pltpu.VMEM((3, ops, quarter, states), BF16),
            pltpu.VMEM((states, states), F32),
            pltpu.VMEM((6, sectors * ops, 8, LANES), F32),
            dma,
            dma,
            dma((sectors, per)),
            dma((sectors, per)),
            dma((3, 3, ops)),
            dma((3, 3, ops)),
            dma((3, ops)),
            dma((3, ops)),
            dma((6, sectors * ops)),
            dma((6, sectors * ops)),
            dma((ops,)),
            dma((ops,)),
        ],
        compiler_params=pltpu.CompilerParams(
            collective_id=0, has_side_effects=True, vmem_limit_bytes=60 * 1024 * 1024
        ),
    )(left_arrival, right, op_charge, sector_dims, wavefunction, onsite)


def solution(mesh):
    in_specs = (
        P(("groups", "sector", "op"), None, None, None),
        P("groups", "op", None, "sector", None, None),
        P("groups"),
        P(("groups", "sector")),
        P(("groups", "sector"), None, None),
        P(("groups", "sector"), None, None),
    )
    out_specs = (P(("groups", "sector"), None, None), P("groups", None))
    return jax.shard_map(
        on_device, mesh=mesh, in_specs=in_specs, out_specs=out_specs, check_vma=False
    )
```
